32 devices in a mesh: tok: 16 (over z, x, core), voc: 2 (over y).
Axes of the slice: x: 2, y: 2, z: 4, core: 2. Of those that a mesh axis runs over, the one named last changes fastest.
Arguments:
- hidden: bfloat16 [2048, 1792], P('tok'), may hold values from -40 to 40
- head_weight: bfloat16 [1792, 16384], P(None, ('voc', 'tok')), may hold values from -0.37796447 to 0.37796447
- teacher_probs: bfloat16 [2048, 16384], P('tok', 'voc'), may hold values from 0 to 1, as said below
- teacher_row: int32 [2048], replicated, may hold values from 0 to 2047, each once
- lengths: int32 [16], replicated, may hold values from 1 to 128, as said below
Outputs:
- head_grad: bfloat16 [1792, 16384], P(None, ('voc', 'tok'))
The draws below stay inside these ranges and needn't reach their ends.
Inputs may be any that keep to these rules, and one draw needn't show every extreme that they name: `teacher_row`: a permutation of the 2048 token positions. `lengths`: the last sequence is full. `teacher_probs`: each row is a probability distribution over the vocabulary: its entries sum to 1 up to rounding.
All inputs are finite; a program needn't handle non-finite values.
Results may differ from the reference program's by a relative error of at most 0.008.
Values may be sent and summed in bfloat16 or wider, within the bound.
A program may use at most 128 MiB of HBM per device.

```python
import jax
import jax.numpy as jnp
from jax import lax

D = 1792
VOC_SUB = 512
SEQ_LEN = 128
TOKENS = 2048
VOCAB = 16384
SEQS = 16


def draw_hidden(key, part):
    key = jax.random.fold_in(key, 1)
    key_rows, key_base = jax.random.split(key, 2)
    row_scale = jnp.exp(jax.random.uniform(key_rows, (TOKENS, 1), jnp.float32, 0.0, jnp.log(10.0)))
    base = jax.random.truncated_normal(key_base, -4.0, 4.0, (TOKENS, D), jnp.float32) * row_scale
    return base.astype(jnp.bfloat16)


def draw_head_weight(key, part):
    key = jax.random.fold_in(key, 2)
    key_cols, key_base = jax.random.split(key)
    col_scale = jnp.exp(jax.random.uniform(key_cols, (VOCAB,), jnp.float32, jnp.log(0.4), jnp.log(4.0)))
    weight = jax.random.truncated_normal(key_base, -4.0, 4.0, (D, VOCAB), jnp.float32) * col_scale[None, :] / jnp.sqrt(jnp.float32(D))
    return weight.astype(jnp.bfloat16)


def draw_teacher_probs(key, part):
    key = jax.random.fold_in(key, 4)
    key_rows, key_vals = jax.random.split(key)
    row_scale = jnp.exp(jax.random.uniform(key_rows, (TOKENS, 1), jnp.float32, jnp.log(2.5), jnp.log(5.0)))
    values = jax.random.truncated_normal(key_vals, -4.5, 4.5, (TOKENS, VOCAB), jnp.float32)
    teacher_logits = values * row_scale
    return jax.nn.softmax(teacher_logits, axis=1).astype(jnp.bfloat16)


def draw_lengths(key, part):
    key = jax.random.fold_in(key, 13)
    index = jnp.arange(SEQS, dtype=jnp.int32)
    lowest = SEQ_LEN // 8 + SEQ_LEN // 2 * index // SEQS
    extra = jax.random.randint(key, (SEQS,), 0, SEQ_LEN // 2 + 1, jnp.int32)
    drawn = jnp.clip(lowest + extra, 1, SEQ_LEN)
    return jnp.where(index == SEQS - 1, SEQ_LEN, drawn).astype(jnp.int32)


def setup_inputs(seed: int = 0) -> dict:
    arg_keys = jax.random.split(jax.random.key(seed), 6)
    hidden = draw_hidden(jax.random.fold_in(arg_keys[5], 71), 0)
    head_weight = draw_head_weight(jax.random.fold_in(arg_keys[5], 71), 0)
    teacher_probs = draw_teacher_probs(jax.random.fold_in(arg_keys[5], 71), 0)
    teacher_row = jax.random.permutation(arg_keys[3], TOKENS).astype(jnp.int32)
    lengths = draw_lengths(jax.random.fold_in(arg_keys[5], 71), 0)
    return {"hidden": hidden, "head_weight": head_weight, "teacher_probs": teacher_probs, "teacher_row": teacher_row, "lengths": lengths}


loss_scale = 1048576.0


def reference(hidden, head_weight, teacher_probs, teacher_row, lengths):
    blocks = VOCAB // VOC_SUB
    weight_blocks = head_weight.reshape(D, blocks, VOC_SUB).transpose(1, 0, 2)
    teacher_blocks = teacher_probs.reshape(TOKENS, blocks, VOC_SUB).transpose(1, 0, 2)

    def stat_step(running, weight_block):
        old_peak, old_total = running
        logits = jnp.dot(hidden, weight_block, preferred_element_type=jnp.float32)
        new_peak = jnp.maximum(old_peak, jnp.max(logits, axis=1))
        new_total = old_total * jnp.exp(old_peak - new_peak) + jnp.sum(jnp.exp(logits - new_peak[:, None]), axis=1)
        return (new_peak, new_total), logits

    start_peak = jnp.full((TOKENS,), -jnp.inf, jnp.float32)
    start_total = jnp.zeros((TOKENS,), jnp.float32)
    (row_peak, row_total), stored = lax.scan(stat_step, (start_peak, start_total), weight_blocks)

    def pieces(logits, teacher_block):
        log_student = (logits - row_peak[:, None]) - jnp.log(row_total)[:, None]
        student = jnp.exp(log_student)
        aligned = jnp.take(teacher_block, teacher_row, axis=0).astype(jnp.float32)
        log_mix = jnp.log(0.5 * aligned + 0.5 * student)
        grad_prob = 0.5 * (log_student - log_mix)
        return student, grad_prob

    def centre_step(running, pair):
        student, grad_prob = pieces(pair[0], pair[1])
        return running + jnp.sum(student * grad_prob, axis=1), None

    centre, unused = lax.scan(centre_step, jnp.zeros((TOKENS,), jnp.float32), (stored, teacher_blocks))
    positions = jnp.arange(TOKENS, dtype=jnp.int32)
    limits = jnp.repeat(lengths, SEQ_LEN, total_repeat_length=TOKENS)
    valid_mask = (positions % SEQ_LEN < limits).astype(jnp.float32)
    token_count = jnp.sum(lengths).astype(jnp.float32)
    grad_scale = loss_scale / token_count

    def grad_block(pair):
        student, grad_prob = pieces(pair[0], pair[1])
        dlogits = (((grad_scale * valid_mask)[:, None] * student) * (grad_prob - centre[:, None])).astype(jnp.bfloat16)
        block_grad = lax.dot_general(hidden, dlogits, (((0,), (0,)), ((), ())), preferred_element_type=jnp.float32)
        return block_grad.astype(jnp.bfloat16)

    grads = lax.map(grad_block, (stored, teacher_blocks))
    return grads.transpose(1, 0, 2).reshape(D, VOCAB)
```

```python
import functools

import jax
import jax.numpy as jnp
from jax import lax
from jax.experimental import pallas as pl
from jax.experimental.pallas import tpu as pltpu
from jax.sharding import PartitionSpec as P

SEQ_LEN = 128
loss_scale = 1048576.0
MESH = pl.DeviceIdType.MESH
F32 = jnp.float32
BF16 = jnp.bfloat16


def head_kernel(
    T, V,
    h_hbm, w_ref, t_hbm, trow_ref, gs_ref, out_ref,
    hbuf, tbuf, tt, wt, logits, student, aligned, dt, xl, xc, comb,
    loc_sem, zs, zr, xs, xr, ys, yr, cs, cr, ts, tr, ls, lr, es, er,
):
    N = T * V
    R, D = h_hbm.shape
    VS = w_ref.shape[1]
    TOK = T * R
    L = T // 4
    part = R // V
    G = R // 128
    me_t, me_v = lax.axis_index("tok"), lax.axis_index("voc")
    me = me_t * V + me_v
    k = lax.rem(me_t, 2)
    x = lax.rem(me_t // 2, 2)
    z = me_t // 4

    def block_of(zz, xx, kk):
        return (zz * 2 + xx) * 2 + kk

    own_h = pltpu.make_async_copy(h_hbm, hbuf.at[pl.ds(pl.multiple_of(me_t * R, R), R), :], loc_sem.at[0])
    own_h.start()
    own_t = pltpu.make_async_copy(
        t_hbm.at[:, pl.ds(pl.multiple_of(me_t * VS, VS), VS)],
        tbuf.at[pl.ds(pl.multiple_of(me_t * R, R), R), :], loc_sem.at[1])
    own_t.start()

    barrier = pltpu.get_barrier_semaphore()

    def greet(i, c):
        to = lax.rem(me + i, N)
        pl.semaphore_signal(barrier, inc=1, device_id=(to // V, lax.rem(to, V)), device_id_type=MESH)
        return c

    lax.fori_loop(1, N, greet, 0)
    own_h.wait()
    pl.semaphore_wait(barrier, N - 1)

    def rows(n, p):
        return hbuf.at[pl.ds(pl.multiple_of(n * R + p * part, part), part), :]

    def whole(n):
        return hbuf.at[pl.ds(pl.multiple_of(n * R, R), R), :]

    def remote(ref, s_sem, r_sem, tok, voc):
        return pltpu.make_async_remote_copy(
            src_ref=ref, dst_ref=ref, send_sem=s_sem, recv_sem=r_sem,
            device_id=(tok, voc), device_id_type=MESH)

    def z_copy(zp, up):
        to = jnp.minimum(z + 1, L - 1) if up else jnp.maximum(z - 1, 0)
        return remote(rows(block_of(zp, x, k), me_v), zs.at[zp, 0 if up else 1], zr.at[zp],
                      block_of(to, x, k), me_v)

    def x_copy(zp):
        return remote(rows(block_of(zp, x, k), me_v), xs.at[zp], xr.at[zp], block_of(z, 1 - x, k), me_v)

    def x_in(zp):
        return remote(rows(block_of(zp, 1 - x, k), me_v), xs.at[zp], xr.at[zp], block_of(z, 1 - x, k), me_v)

    def y_copy(zp, far, j):
        col = 1 - x if far else x
        return remote(rows(block_of(zp, col, k), me_v), ys.at[zp, far, j], yr.at[zp, far, j],
                      me_t, lax.rem(me_v + j, V))

    def y_in(zp, far, j):
        col = 1 - x if far else x
        return remote(rows(block_of(zp, col, k), lax.rem(me_v - j + V, V)), ys.at[zp, far, j], yr.at[zp, far, j],
                      me_t, lax.rem(me_v + j, V))

    def c_copy(zp, far):
        col = 1 - x if far else x
        return remote(whole(block_of(zp, col, k)), cs.at[zp, far], cr.at[zp, far], block_of(z, x, 1 - k), me_v)

    def c_in(zp, far):
        col = 1 - x if far else x
        return remote(whole(block_of(zp, col, 1 - k)), cs.at[zp, far], cr.at[zp, far], block_of(z, x, 1 - k), me_v)

    def t_copy(i):
        to = lax.rem(me_t + i, T)
        return pltpu.make_async_remote_copy(
            src_ref=t_hbm.at[:, pl.ds(pl.multiple_of(to * VS, VS), VS)],
            dst_ref=tbuf.at[pl.ds(pl.multiple_of(me_t * R, R), R), :],
            send_sem=ts.at[i], recv_sem=tr.at[i], device_id=(to, me_v), device_id_type=MESH)

    def t_in(i):
        frm = lax.rem(me_t - i + T, T)
        to = lax.rem(me_t + i, T)
        return pltpu.make_async_remote_copy(
            src_ref=t_hbm.at[:, pl.ds(pl.multiple_of(to * VS, VS), VS)],
            dst_ref=tbuf.at[pl.ds(pl.multiple_of(frm * R, R), R), :],
            send_sem=ts.at[i], recv_sem=tr.at[i], device_id=(to, me_v), device_id_type=MESH)

    def sources(d):
        if d == 0:
            return [(z, None, None)]
        return [(jnp.maximum(z - d, 0), z - d >= 0, True), (jnp.minimum(z + d, L - 1), z + d < L, False)]

    def under(cond, f):
        if cond is None:
            f()
        else:
            pl.when(cond)(f)

    def arrive(d):
        for zp, cond, up in sources(d):
            def f(zp=zp, up=up):
                if d > 0:
                    z_copy(zp, up).wait_recv()
                if d == 0 or up:
                    pl.when(z + 1 < L)(lambda: z_copy(zp, True).start())
                if d == 0 or not up:
                    pl.when(z > 0)(lambda: z_copy(zp, False).start())
                x_copy(zp).start()
                if d == 0:
                    c_copy(zp, 0).start()
                else:
                    for j in range(1, V):
                        y_copy(zp, 0, j).start()
            under(cond, f)

    def crossed(d):
        for zp, cond, up in sources(d):
            def f(zp=zp):
                x_in(zp).wait_recv()
                for j in range(1, V):
                    y_copy(zp, 1, j).start()
            under(cond, f)

    def gathered(d):
        for zp, cond, up in sources(d):
            def f(zp=zp):
                if d > 0:
                    for j in range(1, V):
                        y_in(zp, 0, j).wait_recv()
                    c_copy(zp, 0).start()
                for j in range(1, V):
                    y_in(zp, 1, j).wait_recv()
                c_copy(zp, 1).start()
            under(cond, f)

    arrive(0)

    def t_start(i, c):
        t_copy(i).start()
        return c

    lax.fori_loop(1, T, t_start, 0)

    wt[...] = w_ref[...].astype(F32).T.astype(BF16)

    crossed(0)
    for d in range(1, L):
        arrive(d)
        crossed(d)
        gathered(d - 1)
    gathered(L - 1)

    def c_wait(zp, c):
        c_in(zp, 0).wait_recv()
        c_in(zp, 1).wait_recv()
        return c

    lax.fori_loop(0, L, c_wait, 0)

    CH = 4 * R

    def logit_step(j, c):
        at = pl.ds(pl.multiple_of(j * CH, CH), CH)
        out = lax.dot_general(wt[...], hbuf[at, :], (((1,), (1,)), ((), ())), preferred_element_type=F32)
        logits[:, at] = out
        peak = jnp.max(out, axis=0, keepdims=True)
        lse = peak + jnp.log(jnp.sum(jnp.exp(out - peak), axis=0, keepdims=True))
        for q in range(CH // 128):
            xl[0, pl.ds(j * (CH // 128) + q, 1), :] = lse[:, q * 128:(q + 1) * 128]
        return c

    lax.fori_loop(0, L, logit_step, 0)

    def stat_copy(buf, s, r, i):
        to = lax.rem(me + i, N)
        return pltpu.make_async_remote_copy(
            src_ref=buf.at[0], dst_ref=buf.at[i], send_sem=s.at[i], recv_sem=r.at[i],
            device_id=(to // V, lax.rem(to, V)), device_id_type=MESH)

    def stat_start(buf, s, r):
        def go(i, c):
            stat_copy(buf, s, r, i).start()
            return c
        lax.fori_loop(1, N, go, 0)

    def stat_wait(buf, s, r):
        def go(i, c):
            stat_copy(buf, s, r, i).wait_recv()
            return c
        lax.fori_loop(1, N, go, 0)

    stat_start(xl, ls, lr)

    own_t.wait()

    def transpose_block(frm):
        blk = tbuf[pl.ds(pl.multiple_of(frm * R, R), R), :]
        tt[:, pl.ds(pl.multiple_of(frm * R, R), R)] = blk.astype(F32).T.astype(BF16)

    transpose_block(me_t)

    def t_wait(i, c):
        t_in(i).wait_recv()
        transpose_block(lax.rem(me_t - i + T, T))
        return c

    lax.fori_loop(1, T, t_wait, 0)

    PC = 256

    def align_step(j, c):
        at = pl.ds(pl.multiple_of(j * PC, PC), PC)
        row = trow_ref[:, at]
        hot = jnp.where(lax.broadcasted_iota(jnp.int32, (TOK, PC), 0) == row, 1.0, 0.0).astype(BF16)
        aligned[:, at] = jnp.dot(tt[...], hot, preferred_element_type=F32).astype(BF16)
        return c

    lax.fori_loop(0, TOK // PC, align_step, 0)

    stat_wait(xl, ls, lr)
    peak = jnp.max(xl[...], axis=0)
    comb[...] = peak + jnp.log(jnp.sum(jnp.exp(xl[...] - peak[None]), axis=0))

    def student_step(j, c):
        at = pl.ds(pl.multiple_of(j * 128, 128), 128)
        log_student = logits[:, at] - comb[pl.ds(j, 1), :]
        s = jnp.exp(log_student)
        log_mix = jnp.log(0.5 * aligned[:, at].astype(F32) + 0.5 * s)
        g = 0.5 * (log_student - log_mix)
        logits[:, at] = g
        student[:, at] = s
        xc[0, pl.ds(j, 1), :] = jnp.sum(s * g, axis=0, keepdims=True)
        return c

    lax.fori_loop(0, TOK // 128, student_step, 0)
    stat_start(xc, es, er)
    stat_wait(xc, es, er)
    comb[...] = jnp.sum(xc[...], axis=0)

    def dlogit_step(j, c):
        at = pl.ds(pl.multiple_of(j * 128, 128), 128)
        d = (gs_ref[:, at] * student[:, at]) * (logits[:, at] - comb[pl.ds(j, 1), :])
        dt[:, at] = d.astype(BF16)
        return c

    lax.fori_loop(0, TOK // 128, dlogit_step, 0)

    GC = 256

    def grad_step(j, c):
        at = pl.ds(pl.multiple_of(j * GC, GC), GC)
        g = jnp.dot(dt[...], hbuf[:, at], preferred_element_type=F32)
        out_ref[at, :] = g.T.astype(BF16)
        return c

    lax.fori_loop(0, D // GC, grad_step, 0)

    def drain_stats(i, c):
        stat_copy(xl, ls, lr, i).wait_send()
        stat_copy(xc, es, er, i).wait_send()
        return c

    lax.fori_loop(1, N, drain_stats, 0)

    def drain_teacher(i, c):
        t_copy(i).wait_send()
        return c

    lax.fori_loop(1, T, drain_teacher, 0)

    def drain_hidden(zp, c):
        pl.when((z + 1 < L) & (zp <= z))(lambda: z_copy(zp, True).wait_send())
        pl.when((z > 0) & (zp >= z))(lambda: z_copy(zp, False).wait_send())
        x_copy(zp).wait_send()
        for j in range(1, V):
            y_copy(zp, 1, j).wait_send()
            pl.when(zp != z)(lambda: y_copy(zp, 0, j).wait_send())
        c_copy(zp, 0).wait_send()
        c_copy(zp, 1).wait_send()
        return c

    lax.fori_loop(0, L, drain_hidden, 0)


def per_device(T, V, hidden, head_weight, teacher_probs, teacher_row, lengths):
    R, D = hidden.shape
    VS = head_weight.shape[1]
    TOK = T * R
    N = T * V
    L = T // 4
    valid = jnp.arange(SEQ_LEN, dtype=jnp.int32)[None, :] < lengths[:, None]
    grad_scale = loss_scale / jnp.sum(lengths).astype(F32)
    gs = (grad_scale * valid.astype(F32)).reshape(1, TOK)
    vm = pl.BlockSpec(memory_space=pltpu.VMEM)
    anyspace = pl.BlockSpec(memory_space=pl.ANY)
    dma = pltpu.SemaphoreType.DMA
    return pl.pallas_call(
        functools.partial(head_kernel, T, V),
        out_shape=jax.ShapeDtypeStruct((D, VS), BF16),
        in_specs=[anyspace, vm, anyspace, vm, vm],
        out_specs=vm,
        scratch_shapes=[
            pltpu.VMEM((TOK, D), BF16),
            pltpu.VMEM((TOK, VS), BF16),
            pltpu.VMEM((VS, TOK), BF16),
            pltpu.VMEM((VS, D), BF16),
            pltpu.VMEM((VS, TOK), F32),
            pltpu.VMEM((VS, TOK), F32),
            pltpu.VMEM((VS, TOK), BF16),
            pltpu.VMEM((VS, TOK), BF16),
            pltpu.VMEM((N, TOK // 128, 128), F32),
            pltpu.VMEM((N, TOK // 128, 128), F32),
            pltpu.VMEM((TOK // 128, 128), F32),
            dma((2,)),
            dma((L, 2)), dma((L,)),
            dma((L,)), dma((L,)),
            dma((L, 2, V)), dma((L, 2, V)),
            dma((L, 2)), dma((L, 2)),
            dma((T,)), dma((T,)),
            dma((N,)), dma((N,)),
            dma((N,)), dma((N,)),
        ],
        compiler_params=pltpu.CompilerParams(
            collective_id=0, has_side_effects=True, vmem_limit_bytes=60 * 1024 * 1024
        ),
        cost_estimate=pl.CostEstimate(
            flops=6 * TOK * D * VS, bytes_accessed=4 * TOK * D, transcendentals=4 * TOK * VS
        ),
        name="head_grad",
    )(hidden, head_weight, teacher_probs, teacher_row.reshape(1, TOK), gs)


def solution(mesh):
    return jax.shard_map(
        functools.partial(per_device, mesh.shape["tok"], mesh.shape["voc"]),
        mesh=mesh,
        in_specs=(P("tok", None), P(None, ("voc", "tok")), P("tok", "voc"), P(), P()),
        out_specs=P(None, ("voc", "tok")),
        check_vma=False,
    )
```

```python
import functools

import jax
import jax.numpy as jnp
from jax import lax
from jax.experimental import pallas as pl
from jax.experimental.pallas import tpu as pltpu
from jax.sharding import PartitionSpec as P

SEQ_LEN = 128
loss_scale = 1048576.0
MESH = pl.DeviceIdType.MESH
F32 = jnp.float32
BF16 = jnp.bfloat16


def head_kernel(
    T, V,
    h_hbm, w_hbm, t_hbm, trow_ref, len_ref, out_ref,
    wbuf, hot, hbuf, tbuf, tt, wt, logits, student, aligned, dt, xl, xc, comb,
    loc_sem, zs, zr, xs, xr, ys, yr, cs, cr, ts, tr, ls, lr, es, er,
):
    N = T * V
    R, D = h_hbm.shape
    VS = w_hbm.shape[1]
    TOK = T * R
    L = T // 4
    part = R // V
    me_t, me_v = lax.axis_index("tok"), lax.axis_index("voc")
    me = me_t * V + me_v
    k = lax.rem(me_t, 2)
    x = lax.rem(me_t // 2, 2)
    z = me_t // 4

    def block_of(zz, xx, kk):
        return (zz * 2 + xx) * 2 + kk

    own_h = pltpu.make_async_copy(h_hbm, hbuf.at[pl.ds(pl.multiple_of(me_t * R, R), R), :], loc_sem.at[0])
    own_h.start()
    own_t = pltpu.make_async_copy(
        t_hbm.at[:, pl.ds(pl.multiple_of(me_t * VS, VS), VS)],
        tbuf.at[pl.ds(pl.multiple_of(me_t * R, R), R), :], loc_sem.at[1])
    own_t.start()

    own_w = pltpu.make_async_copy(w_hbm, wbuf, loc_sem.at[2])
    own_w.start()

    barrier = pltpu.get_barrier_semaphore()

    def greet(i, c):
        to = lax.rem(me + i, N)
        pl.semaphore_signal(barrier, inc=1, device_id=(to // V, lax.rem(to, V)), device_id_type=MESH)
        return c

    lax.fori_loop(1, N, greet, 0)
    own_h.wait()
    pl.semaphore_wait(barrier, N - 1)

    def rows(n, p):
        return hbuf.at[pl.ds(pl.multiple_of(n * R + p * part, part), part), :]

    def whole(n):
        return hbuf.at[pl.ds(pl.multiple_of(n * R, R), R), :]

    def remote(ref, s_sem, r_sem, tok, voc):
        return pltpu.make_async_remote_copy(
            src_ref=ref, dst_ref=ref, send_sem=s_sem, recv_sem=r_sem,
            device_id=(tok, voc), device_id_type=MESH)

    def z_copy(zp, up):
        to = jnp.minimum(z + 1, L - 1) if up else jnp.maximum(z - 1, 0)
        return remote(rows(block_of(zp, x, k), me_v), zs.at[zp, 0 if up else 1], zr.at[zp],
                      block_of(to, x, k), me_v)

    def x_copy(zp):
        return remote(rows(block_of(zp, x, k), me_v), xs.at[zp], xr.at[zp], block_of(z, 1 - x, k), me_v)

    def x_in(zp):
        return remote(rows(block_of(zp, 1 - x, k), me_v), xs.at[zp], xr.at[zp], block_of(z, 1 - x, k), me_v)

    def y_copy(zp, far, j):
        col = 1 - x if far else x
        return remote(rows(block_of(zp, col, k), me_v), ys.at[zp, far, j], yr.at[zp, far, j],
                      me_t, lax.rem(me_v + j, V))

    def y_in(zp, far, j):
        col = 1 - x if far else x
        return remote(rows(block_of(zp, col, k), lax.rem(me_v - j + V, V)), ys.at[zp, far, j], yr.at[zp, far, j],
                      me_t, lax.rem(me_v + j, V))

    def c_copy(zp, far):
        col = 1 - x if far else x
        return remote(whole(block_of(zp, col, k)), cs.at[zp, far], cr.at[zp, far], block_of(z, x, 1 - k), me_v)

    def c_in(zp, far):
        col = 1 - x if far else x
        return remote(whole(block_of(zp, col, 1 - k)), cs.at[zp, far], cr.at[zp, far], block_of(z, x, 1 - k), me_v)

    def t_copy(i):
        to = lax.rem(me_t + i, T)
        return pltpu.make_async_remote_copy(
            src_ref=t_hbm.at[:, pl.ds(pl.multiple_of(to * VS, VS), VS)],
            dst_ref=tbuf.at[pl.ds(pl.multiple_of(me_t * R, R), R), :],
            send_sem=ts.at[i], recv_sem=tr.at[i], device_id=(to, me_v), device_id_type=MESH)

    def t_in(i):
        frm = lax.rem(me_t - i + T, T)
        to = lax.rem(me_t + i, T)
        return pltpu.make_async_remote_copy(
            src_ref=t_hbm.at[:, pl.ds(pl.multiple_of(to * VS, VS), VS)],
            dst_ref=tbuf.at[pl.ds(pl.multiple_of(frm * R, R), R), :],
            send_sem=ts.at[i], recv_sem=tr.at[i], device_id=(to, me_v), device_id_type=MESH)

    def sources(d):
        if d == 0:
            return [(z, None, None)]
        return [(jnp.maximum(z - d, 0), z - d >= 0, True), (jnp.minimum(z + d, L - 1), z + d < L, False)]

    def under(cond, f):
        if cond is None:
            f()
        else:
            pl.when(cond)(f)

    def arrive(d):
        for zp, cond, up in sources(d):
            def f(zp=zp, up=up):
                if d > 0:
                    z_copy(zp, up).wait_recv()
                if d == 0 or up:
                    pl.when(z + 1 < L)(lambda: z_copy(zp, True).start())
                if d == 0 or not up:
                    pl.when(z > 0)(lambda: z_copy(zp, False).start())
                x_copy(zp).start()
                if d == 0:
                    c_copy(zp, 0).start()
                else:
                    for j in range(1, V):
                        y_copy(zp, 0, j).start()
            under(cond, f)

    def crossed(d):
        for zp, cond, up in sources(d):
            def f(zp=zp):
                x_in(zp).wait_recv()
                for j in range(1, V):
                    y_copy(zp, 1, j).start()
            under(cond, f)

    def gathered(d):
        for zp, cond, up in sources(d):
            def f(zp=zp):
                if d > 0:
                    for j in range(1, V):
                        y_in(zp, 0, j).wait_recv()
                    c_copy(zp, 0).start()
                for j in range(1, V):
                    y_in(zp, 1, j).wait_recv()
                c_copy(zp, 1).start()
            under(cond, f)

    def t_start(i, c):
        to_z = lax.rem(me_t + i, T) // 4
        far = to_z != z
        pl.when(far if c else jnp.logical_not(far))(lambda: t_copy(i).start())

    def t_starts(across):
        def go(i, c):
            t_start(i, across)
            return c
        lax.fori_loop(1, T, go, 0)

    HC = 256

    def hot_chunk(j):
        row = trow_ref[:, pl.ds(pl.multiple_of(j * HC, HC), HC)]
        return jnp.where(lax.broadcasted_iota(jnp.int32, (TOK, HC), 0) == row, 1.0, 0.0).astype(BF16)

    keep_hot = hot.shape[1] == TOK

    arrive(0)
    t_starts(False)
    own_w.wait()
    wt[...] = wbuf[...].astype(F32).T.astype(BF16)
    arrive(1)
    crossed(0)
    for d in range(2, L):
        arrive(d)
        crossed(d - 1)
    t_starts(True)
    if keep_hot:
        def hot_step(j, c):
            hot[:, pl.ds(pl.multiple_of(j * HC, HC), HC)] = hot_chunk(j)
            return c
        lax.fori_loop(0, TOK // HC // 2, hot_step, 0)
    gathered(0)
    crossed(L - 1)
    for d in range(1, L):
        gathered(d)
    if keep_hot:
        lax.fori_loop(TOK // HC // 2, TOK // HC, hot_step, 0)

    def c_wait(zp, c):
        c_in(zp, 0).wait_recv()
        c_in(zp, 1).wait_recv()
        return c

    lax.fori_loop(0, L, c_wait, 0)

    CH = 4 * R

    def logit_step(j, c):
        at = pl.ds(pl.multiple_of(j * CH, CH), CH)
        out = lax.dot_general(wt[...], hbuf[at, :], (((1,), (1,)), ((), ())), preferred_element_type=F32)
        logits[:, at] = out
        peak = jnp.max(out, axis=0, keepdims=True)
        lse = peak + jnp.log(jnp.sum(jnp.exp(out - peak), axis=0, keepdims=True))
        for q in range(CH // 128):
            xl[0, pl.ds(j * (CH // 128) + q, 1), :] = lse[:, q * 128:(q + 1) * 128]
        return c

    lax.fori_loop(0, L, logit_step, 0)

    def stat_copy(buf, s, r, i):
        to = lax.rem(me + i, N)
        return pltpu.make_async_remote_copy(
            src_ref=buf.at[0], dst_ref=buf.at[i], send_sem=s.at[i], recv_sem=r.at[i],
            device_id=(to // V, lax.rem(to, V)), device_id_type=MESH)

    def stat_start(buf, s, r):
        def go(i, c):
            stat_copy(buf, s, r, i).start()
            return c
        lax.fori_loop(1, N, go, 0)

    def stat_wait(buf, s, r):
        def go(i, c):
            stat_copy(buf, s, r, i).wait_recv()
            return c
        lax.fori_loop(1, N, go, 0)

    stat_start(xl, ls, lr)

    own_t.wait()

    def transpose_block(frm):
        blk = tbuf[pl.ds(pl.multiple_of(frm * R, R), R), :]
        tt[:, pl.ds(pl.multiple_of(frm * R, R), R)] = blk.astype(F32).T.astype(BF16)

    transpose_block(me_t)

    def t_wait(i, c):
        t_in(i).wait_recv()
        transpose_block(lax.rem(me_t - i + T, T))
        return c

    lax.fori_loop(1, T, t_wait, 0)

    def align_step(j, c):
        at = pl.ds(pl.multiple_of(j * HC, HC), HC)
        pick = hot[:, at] if keep_hot else hot_chunk(j)
        aligned[:, at] = jnp.dot(tt[...], pick, preferred_element_type=F32).astype(BF16)
        return c

    lax.fori_loop(0, TOK // HC, align_step, 0)

    stat_wait(xl, ls, lr)
    peak = jnp.max(xl[...], axis=0)
    comb[...] = peak + jnp.log(jnp.sum(jnp.exp(xl[...] - peak[None]), axis=0))

    def student_step(j, c):
        at = pl.ds(pl.multiple_of(j * 128, 128), 128)
        log_student = logits[:, at] - comb[pl.ds(j, 1), :]
        s = jnp.exp(log_student)
        log_mix = jnp.log(0.5 * aligned[:, at].astype(F32) + 0.5 * s)
        g = 0.5 * (log_student - log_mix)
        logits[:, at] = g
        student[:, at] = s
        xc[0, pl.ds(j, 1), :] = jnp.sum(s * g, axis=0, keepdims=True)
        return c

    lax.fori_loop(0, TOK // 128, student_step, 0)
    stat_start(xc, es, er)
    stat_wait(xc, es, er)
    comb[...] = jnp.sum(xc[...], axis=0)

    count = lax.fori_loop(0, TOK // SEQ_LEN, lambda j, c: c + len_ref[j], jnp.int32(0))
    grad_scale = loss_scale / jnp.full((1, SEQ_LEN), count, jnp.int32).astype(F32)
    slot = lax.broadcasted_iota(jnp.int32, (1, SEQ_LEN), 1)

    def dlogit_step(j, c):
        at = pl.ds(pl.multiple_of(j * SEQ_LEN, SEQ_LEN), SEQ_LEN)
        scale = jnp.where(slot < len_ref[j], grad_scale, 0.0)
        d = (scale * student[:, at]) * (logits[:, at] - comb[pl.ds(j, 1), :])
        dt[:, at] = d.astype(BF16)
        return c

    lax.fori_loop(0, TOK // 128, dlogit_step, 0)

    GC = 256

    def grad_step(j, c):
        at = pl.ds(pl.multiple_of(j * GC, GC), GC)
        g = jnp.dot(dt[...], hbuf[:, at], preferred_element_type=F32)
        out_ref[at, :] = g.T.astype(BF16)
        return c

    lax.fori_loop(0, D // GC, grad_step, 0)

    def drain_stats(i, c):
        stat_copy(xl, ls, lr, i).wait_send()
        stat_copy(xc, es, er, i).wait_send()
        return c

    lax.fori_loop(1, N, drain_stats, 0)

    def drain_teacher(i, c):
        t_copy(i).wait_send()
        return c

    lax.fori_loop(1, T, drain_teacher, 0)

    def drain_hidden(zp, c):
        pl.when((z + 1 < L) & (zp <= z))(lambda: z_copy(zp, True).wait_send())
        pl.when((z > 0) & (zp >= z))(lambda: z_copy(zp, False).wait_send())
        x_copy(zp).wait_send()
        for j in range(1, V):
            y_copy(zp, 1, j).wait_send()
            pl.when(zp != z)(lambda: y_copy(zp, 0, j).wait_send())
        c_copy(zp, 0).wait_send()
        c_copy(zp, 1).wait_send()
        return c

    lax.fori_loop(0, L, drain_hidden, 0)


def per_device(T, V, hidden, head_weight, teacher_probs, teacher_row, lengths):
    R, D = hidden.shape
    VS = head_weight.shape[1]
    TOK = T * R
    N = T * V
    L = T // 4
    vm = pl.BlockSpec(memory_space=pltpu.VMEM)
    anyspace = pl.BlockSpec(memory_space=pl.ANY)
    dma = pltpu.SemaphoreType.DMA
    return pl.pallas_call(
        functools.partial(head_kernel, T, V),
        out_shape=jax.ShapeDtypeStruct((D, VS), BF16),
        in_specs=[anyspace, anyspace, anyspace, vm, pl.BlockSpec(memory_space=pltpu.SMEM)],
        out_specs=vm,
        scratch_shapes=[
            pltpu.VMEM((D, VS), BF16),
            pltpu.VMEM((TOK, TOK) if TOK * TOK <= 2**22 else (16, 128), BF16),
            pltpu.VMEM((TOK, D), BF16),
            pltpu.VMEM((TOK, VS), BF16),
            pltpu.VMEM((VS, TOK), BF16),
            pltpu.VMEM((VS, D), BF16),
            pltpu.VMEM((VS, TOK), F32),
            pltpu.VMEM((VS, TOK), F32),
            pltpu.VMEM((VS, TOK), BF16),
            pltpu.VMEM((VS, TOK), BF16),
            pltpu.VMEM((N, TOK // 128, 128), F32),
            pltpu.VMEM((N, TOK // 128, 128), F32),
            pltpu.VMEM((TOK // 128, 128), F32),
            dma((3,)),
            dma((L, 2)), dma((L,)),
            dma((L,)), dma((L,)),
            dma((L, 2, V)), dma((L, 2, V)),
            dma((L, 2)), dma((L, 2)),
            dma((T,)), dma((T,)),
            dma((N,)), dma((N,)),
            dma((N,)), dma((N,)),
        ],
        compiler_params=pltpu.CompilerParams(
            collective_id=0, has_side_effects=True, vmem_limit_bytes=60 * 1024 * 1024
        ),
        cost_estimate=pl.CostEstimate(
            flops=6 * TOK * D * VS, bytes_accessed=4 * TOK * D, transcendentals=4 * TOK * VS
        ),
        name="head_grad",
    )(hidden, head_weight, teacher_probs, teacher_row.reshape(1, TOK), lengths)


def solution(mesh):
    return jax.shard_map(
        functools.partial(per_device, mesh.shape["tok"], mesh.shape["voc"]),
        mesh=mesh,
        in_specs=(P("tok", None), P(None, ("voc", "tok")), P("tok", "voc"), P(), P()),
        out_specs=P(None, ("voc", "tok")),
        check_vma=False,
    )
```

```python
import functools

import jax
import jax.numpy as jnp
from jax import lax
from jax.experimental import pallas as pl
from jax.experimental.pallas import tpu as pltpu
from jax.sharding import PartitionSpec as P

SEQ_LEN = 128
loss_scale = 1048576.0
MESH = pl.DeviceIdType.MESH
F32 = jnp.float32
BF16 = jnp.bfloat16


def head_kernel(
    T, V,
    h_hbm, w_hbm, t_hbm, trow_ref, len_ref, out_ref,
    wbuf, hot, hbuf, tload, tsend, tt, wt, logits, student, dt, xl, xc, comb,
    loc_sem, zs, zr, xs, xr, ys, yr, cs, cr, ts, tr, ls, lr, es, er,
):
    N = T * V
    R, D = h_hbm.shape
    VS = w_hbm.shape[1]
    TOK = T * R
    L = T // 4
    part = R // V
    me_t, me_v = lax.axis_index("tok"), lax.axis_index("voc")
    me = me_t * V + me_v
    k = lax.rem(me_t, 2)
    x = lax.rem(me_t // 2, 2)
    z = me_t // 4

    def block_of(zz, xx, kk):
        return (zz * 2 + xx) * 2 + kk

    own_h = pltpu.make_async_copy(h_hbm, hbuf.at[pl.ds(pl.multiple_of(me_t * R, R), R), :], loc_sem.at[0])
    own_h.start()
    own_t = pltpu.make_async_copy(t_hbm, tload, loc_sem.at[1])
    own_t.start()

    own_w = pltpu.make_async_copy(w_hbm, wbuf, loc_sem.at[2])
    own_w.start()

    barrier = pltpu.get_barrier_semaphore()

    def greet(i, c):
        to = lax.rem(me + i, N)
        pl.semaphore_signal(barrier, inc=1, device_id=(to // V, lax.rem(to, V)), device_id_type=MESH)
        return c

    lax.fori_loop(1, N, greet, 0)
    own_h.wait()
    pl.semaphore_wait(barrier, N - 1)

    def rows(n, p):
        return hbuf.at[pl.ds(pl.multiple_of(n * R + p * part, part), part), :]

    def whole(n):
        return hbuf.at[pl.ds(pl.multiple_of(n * R, R), R), :]

    def remote(ref, s_sem, r_sem, tok, voc):
        return pltpu.make_async_remote_copy(
            src_ref=ref, dst_ref=ref, send_sem=s_sem, recv_sem=r_sem,
            device_id=(tok, voc), device_id_type=MESH)

    def z_copy(zp, up):
        to = jnp.minimum(z + 1, L - 1) if up else jnp.maximum(z - 1, 0)
        return remote(rows(block_of(zp, x, k), me_v), zs.at[zp, 0 if up else 1], zr.at[zp],
                      block_of(to, x, k), me_v)

    def x_copy(zp):
        return remote(rows(block_of(zp, x, k), me_v), xs.at[zp], xr.at[zp], block_of(z, 1 - x, k), me_v)

    def x_in(zp):
        return remote(rows(block_of(zp, 1 - x, k), me_v), xs.at[zp], xr.at[zp], block_of(z, 1 - x, k), me_v)

    def y_copy(zp, far, j):
        col = 1 - x if far else x
        return remote(rows(block_of(zp, col, k), me_v), ys.at[zp, far, j], yr.at[zp, far, j],
                      me_t, lax.rem(me_v + j, V))

    def y_in(zp, far, j):
        col = 1 - x if far else x
        return remote(rows(block_of(zp, col, k), lax.rem(me_v - j + V, V)), ys.at[zp, far, j], yr.at[zp, far, j],
                      me_t, lax.rem(me_v + j, V))

    def c_copy(zp, far):
        col = 1 - x if far else x
        return remote(whole(block_of(zp, col, k)), cs.at[zp, far], cr.at[zp, far], block_of(z, x, 1 - k), me_v)

    def c_in(zp, far):
        col = 1 - x if far else x
        return remote(whole(block_of(zp, col, 1 - k)), cs.at[zp, far], cr.at[zp, far], block_of(z, x, 1 - k), me_v)

    def t_copy(i, frm=me_t):
        to = lax.rem(me_t + i, T)
        return pltpu.make_async_remote_copy(
            src_ref=tsend.at[pl.ds(pl.multiple_of(to * VS, VS), VS), :],
            dst_ref=tt.at[:, pl.ds(pl.multiple_of(frm * R, R), R)],
            send_sem=ts.at[i], recv_sem=tr.at[i], device_id=(to, me_v), device_id_type=MESH)

    def t_in(i):
        return t_copy(i, lax.rem(me_t - i + T, T))

    def sources(d):
        if d == 0:
            return [(z, None, None)]
        return [(jnp.maximum(z - d, 0), z - d >= 0, True), (jnp.minimum(z + d, L - 1), z + d < L, False)]

    def under(cond, f):
        if cond is None:
            f()
        else:
            pl.when(cond)(f)

    def arrive(d):
        for zp, cond, up in sources(d):
            def f(zp=zp, up=up):
                if d > 0:
                    z_copy(zp, up).wait_recv()
                if d == 0 or up:
                    pl.when(z + 1 < L)(lambda: z_copy(zp, True).start())
                if d == 0 or not up:
                    pl.when(z > 0)(lambda: z_copy(zp, False).start())
                x_copy(zp).start()
                if d == 0:
                    c_copy(zp, 0).start()
                else:
                    for j in range(1, V):
                        y_copy(zp, 0, j).start()
            under(cond, f)

    def crossed(d):
        for zp, cond, up in sources(d):
            def f(zp=zp):
                x_in(zp).wait_recv()
                for j in range(1, V):
                    y_copy(zp, 1, j).start()
            under(cond, f)

    def gathered(d):
        for zp, cond, up in sources(d):
            def f(zp=zp):
                if d > 0:
                    for j in range(1, V):
                        y_in(zp, 0, j).wait_recv()
                    c_copy(zp, 0).start()
                for j in range(1, V):
                    y_in(zp, 1, j).wait_recv()
                c_copy(zp, 1).start()
            under(cond, f)

    def t_start(i, c):
        to_z = lax.rem(me_t + i, T) // 4
        far = to_z != z
        pl.when(far if c else jnp.logical_not(far))(lambda: t_copy(i).start())

    def t_starts(across):
        def go(i, c):
            t_start(i, across)
            return c
        lax.fori_loop(1, T, go, 0)

    HC = 256

    def hot_chunk(j):
        row = trow_ref[:, pl.ds(pl.multiple_of(j * HC, HC), HC)]
        return jnp.where(lax.broadcasted_iota(jnp.int32, (TOK, HC), 0) == row, 1.0, 0.0).astype(BF16)

    keep_hot = hot.shape[1] == TOK

    def turn_step(j, c):
        at = pl.ds(pl.multiple_of(j * VS, VS), VS)
        tsend[at, :] = tload[:, at].astype(F32).T.astype(BF16)
        return c

    arrive(0)
    own_t.wait()
    lax.fori_loop(0, T, turn_step, 0)
    t_starts(False)
    mine = pl.ds(pl.multiple_of(me_t * R, R), R)
    tt[:, mine] = tsend[pl.ds(pl.multiple_of(me_t * VS, VS), VS), :]
    own_w.wait()
    wt[...] = wbuf[...].astype(F32).T.astype(BF16)
    arrive(1)
    crossed(0)
    for d in range(2, L):
        arrive(d)
        crossed(d - 1)
    t_starts(True)
    if keep_hot:
        def hot_step(j, c):
            hot[:, pl.ds(pl.multiple_of(j * HC, HC), HC)] = hot_chunk(j)
            return c
        lax.fori_loop(0, TOK // HC // 2, hot_step, 0)
    gathered(0)
    crossed(L - 1)
    for d in range(1, L):
        gathered(d)
    if keep_hot:
        lax.fori_loop(TOK // HC // 2, TOK // HC, hot_step, 0)

    def c_wait(zp, c):
        c_in(zp, 0).wait_recv()
        c_in(zp, 1).wait_recv()
        return c

    lax.fori_loop(0, L, c_wait, 0)

    CH = 4 * R

    def logit_step(j, c):
        at = pl.ds(pl.multiple_of(j * CH, CH), CH)
        out = lax.dot_general(wt[...], hbuf[at, :], (((1,), (1,)), ((), ())), preferred_element_type=F32)
        logits[:, at] = out
        peak = jnp.max(out, axis=0, keepdims=True)
        lse = peak + jnp.log(jnp.sum(jnp.exp(out - peak), axis=0, keepdims=True))
        for q in range(CH // 128):
            xl[0, pl.ds(j * (CH // 128) + q, 1), :] = lse[:, q * 128:(q + 1) * 128]
        return c

    lax.fori_loop(0, L, logit_step, 0)

    def stat_copy(buf, s, r, i):
        to = lax.rem(me + i, N)
        return pltpu.make_async_remote_copy(
            src_ref=buf.at[0], dst_ref=buf.at[i], send_sem=s.at[i], recv_sem=r.at[i],
            device_id=(to // V, lax.rem(to, V)), device_id_type=MESH)

    def stat_start(buf, s, r):
        def go(i, c):
            stat_copy(buf, s, r, i).start()
            return c
        lax.fori_loop(1, N, go, 0)

    def stat_wait(buf, s, r):
        def go(i, c):
            stat_copy(buf, s, r, i).wait_recv()
            return c
        lax.fori_loop(1, N, go, 0)

    stat_start(xl, ls, lr)

    def t_wait(i, c):
        t_in(i).wait_recv()
        return c

    lax.fori_loop(1, T, t_wait, 0)

    stat_wait(xl, ls, lr)
    peak = jnp.max(xl[...], axis=0)
    comb[...] = peak + jnp.log(jnp.sum(jnp.exp(xl[...] - peak[None]), axis=0))

    for j in range(TOK // HC):
        pick = hot[:, j * HC:(j + 1) * HC] if keep_hot else hot_chunk(j)
        aligned = jnp.dot(tt[...], pick, preferred_element_type=F32)
        for q in range(HC // 128):
            row = j * (HC // 128) + q
            at = slice(row * 128, (row + 1) * 128)
            log_student = logits[:, at] - comb[row:row + 1, :]
            s = jnp.exp(log_student)
            log_mix = jnp.log(0.5 * aligned[:, q * 128:(q + 1) * 128] + 0.5 * s)
            g = 0.5 * (log_student - log_mix)
            logits[:, at] = g
            student[:, at] = s
            xc[0, row:row + 1, :] = jnp.sum(s * g, axis=0, keepdims=True)

    stat_start(xc, es, er)
    stat_wait(xc, es, er)
    comb[...] = jnp.sum(xc[...], axis=0)

    count = lax.fori_loop(0, TOK // SEQ_LEN, lambda j, c: c + len_ref[j], jnp.int32(0))
    grad_scale = loss_scale / jnp.full((1, SEQ_LEN), count, jnp.int32).astype(F32)
    slot = lax.broadcasted_iota(jnp.int32, (1, SEQ_LEN), 1)

    def dlogit_step(j, c):
        at = pl.ds(pl.multiple_of(j * SEQ_LEN, SEQ_LEN), SEQ_LEN)
        scale = jnp.where(slot < len_ref[j], grad_scale, 0.0)
        d = (scale * student[:, at]) * (logits[:, at] - comb[pl.ds(j, 1), :])
        dt[:, at] = d.astype(BF16)
        return c

    lax.fori_loop(0, TOK // 128, dlogit_step, 0)

    GC = 256

    for j in range(D // GC):
        at = slice(j * GC, (j + 1) * GC)
        g = jnp.dot(dt[...], hbuf[:, at], preferred_element_type=F32)
        out_ref[at, :] = g.T.astype(BF16)

    def drain_stats(i, c):
        stat_copy(xl, ls, lr, i).wait_send()
        stat_copy(xc, es, er, i).wait_send()
        return c

    lax.fori_loop(1, N, drain_stats, 0)

    def drain_teacher(i, c):
        t_copy(i).wait_send()
        return c

    lax.fori_loop(1, T, drain_teacher, 0)

    def drain_hidden(zp, c):
        pl.when((z + 1 < L) & (zp <= z))(lambda: z_copy(zp, True).wait_send())
        pl.when((z > 0) & (zp >= z))(lambda: z_copy(zp, False).wait_send())
        x_copy(zp).wait_send()
        for j in range(1, V):
            y_copy(zp, 1, j).wait_send()
            pl.when(zp != z)(lambda: y_copy(zp, 0, j).wait_send())
        c_copy(zp, 0).wait_send()
        c_copy(zp, 1).wait_send()
        return c

    lax.fori_loop(0, L, drain_hidden, 0)


def per_device(T, V, hidden, head_weight, teacher_probs, teacher_row, lengths):
    R, D = hidden.shape
    VS = head_weight.shape[1]
    TOK = T * R
    N = T * V
    L = T // 4
    vm = pl.BlockSpec(memory_space=pltpu.VMEM)
    anyspace = pl.BlockSpec(memory_space=pl.ANY)
    dma = pltpu.SemaphoreType.DMA
    return pl.pallas_call(
        functools.partial(head_kernel, T, V),
        out_shape=jax.ShapeDtypeStruct((D, VS), BF16),
        in_specs=[anyspace, anyspace, anyspace, vm, pl.BlockSpec(memory_space=pltpu.SMEM)],
        out_specs=vm,
        scratch_shapes=[
            pltpu.VMEM((D, VS), BF16),
            pltpu.VMEM((TOK, TOK) if TOK * TOK <= 2**22 else (16, 128), BF16),
            pltpu.VMEM((TOK, D), BF16),
            pltpu.VMEM((R, T * VS), BF16),
            pltpu.VMEM((T * VS, R), BF16),
            pltpu.VMEM((VS, TOK), BF16),
            pltpu.VMEM((VS, D), BF16),
            pltpu.VMEM((VS, TOK), F32),
            pltpu.VMEM((VS, TOK), F32),
            pltpu.VMEM((VS, TOK), BF16),
            pltpu.VMEM((N, TOK // 128, 128), F32),
            pltpu.VMEM((N, TOK // 128, 128), F32),
            pltpu.VMEM((TOK // 128, 128), F32),
            dma((3,)),
            dma((L, 2)), dma((L,)),
            dma((L,)), dma((L,)),
            dma((L, 2, V)), dma((L, 2, V)),
            dma((L, 2)), dma((L, 2)),
            dma((T,)), dma((T,)),
            dma((N,)), dma((N,)),
            dma((N,)), dma((N,)),
        ],
        compiler_params=pltpu.CompilerParams(
            collective_id=0, has_side_effects=True, vmem_limit_bytes=60 * 1024 * 1024
        ),
        cost_estimate=pl.CostEstimate(
            flops=6 * TOK * D * VS, bytes_accessed=4 * TOK * D, transcendentals=4 * TOK * VS
        ),
        name="head_grad",
    )(hidden, head_weight, teacher_probs, teacher_row.reshape(1, TOK), lengths)


def solution(mesh):
    return jax.shard_map(
        functools.partial(per_device, mesh.shape["tok"], mesh.shape["voc"]),
        mesh=mesh,
        in_specs=(P("tok", None), P(None, ("voc", "tok")), P("tok", "voc"), P(), P()),
        out_specs=P(None, ("voc", "tok")),
        check_vma=False,
    )
```

```python
import functools

import jax
import jax.numpy as jnp
from jax import lax
from jax.experimental import pallas as pl
from jax.experimental.pallas import tpu as pltpu
from jax.sharding import PartitionSpec as P

SEQ_LEN = 128
loss_scale = 1048576.0
MESH = pl.DeviceIdType.MESH
F32 = jnp.float32
BF16 = jnp.bfloat16


def head_kernel(
    T, V,
    h_hbm, w_hbm, t_hbm, trow_ref, len_ref, out_ref,
    wbuf, hot, hbuf, tload, tsend, tt, wt, logits, student, dt, xl, xc, comb,
    loc_sem, zs, zr, xs, xr, ys, yr, cs, cr, ts, tr, ls, lr, es, er,
):
    N = T * V
    R, D = h_hbm.shape
    VS = w_hbm.shape[1]
    TOK = T * R
    L = T // 4
    part = R // V
    me_t, me_v = lax.axis_index("tok"), lax.axis_index("voc")
    me = me_t * V + me_v
    k = lax.rem(me_t, 2)
    x = lax.rem(me_t // 2, 2)
    z = me_t // 4

    def block_of(zz, xx, kk):
        return (zz * 2 + xx) * 2 + kk

    own_h = pltpu.make_async_copy(h_hbm, hbuf.at[pl.ds(pl.multiple_of(me_t * R, R), R), :], loc_sem.at[0])
    own_h.start()
    own_t = pltpu.make_async_copy(t_hbm, tload, loc_sem.at[1])
    own_t.start()

    own_w = pltpu.make_async_copy(w_hbm, wbuf, loc_sem.at[2])
    own_w.start()

    barrier = pltpu.get_barrier_semaphore()

    def greet(i, c):
        to = lax.rem(me + i, N)
        pl.semaphore_signal(barrier, inc=1, device_id=(to // V, lax.rem(to, V)), device_id_type=MESH)
        return c

    lax.fori_loop(1, N, greet, 0)
    own_h.wait()
    pl.semaphore_wait(barrier, N - 1)

    def rows(n, p):
        return hbuf.at[pl.ds(pl.multiple_of(n * R + p * part, part), part), :]

    def whole(n):
        return hbuf.at[pl.ds(pl.multiple_of(n * R, R), R), :]

    def remote(ref, s_sem, r_sem, tok, voc):
        return pltpu.make_async_remote_copy(
            src_ref=ref, dst_ref=ref, send_sem=s_sem, recv_sem=r_sem,
            device_id=(tok, voc), device_id_type=MESH)

    def z_copy(zp, up):
        to = jnp.minimum(z + 1, L - 1) if up else jnp.maximum(z - 1, 0)
        return remote(rows(block_of(zp, x, k), me_v), zs.at[zp, 0 if up else 1], zr.at[zp],
                      block_of(to, x, k), me_v)

    def x_copy(zp):
        return remote(rows(block_of(zp, x, k), me_v), xs.at[zp], xr.at[zp], block_of(z, 1 - x, k), me_v)

    def x_in(zp):
        return remote(rows(block_of(zp, 1 - x, k), me_v), xs.at[zp], xr.at[zp], block_of(z, 1 - x, k), me_v)

    def y_copy(zp, far, j):
        col = 1 - x if far else x
        return remote(rows(block_of(zp, col, k), me_v), ys.at[zp, far, j], yr.at[zp, far, j],
                      me_t, lax.rem(me_v + j, V))

    def y_in(zp, far, j):
        col = 1 - x if far else x
        return remote(rows(block_of(zp, col, k), lax.rem(me_v - j + V, V)), ys.at[zp, far, j], yr.at[zp, far, j],
                      me_t, lax.rem(me_v + j, V))

    def c_copy(zp, far):
        col = 1 - x if far else x
        return remote(whole(block_of(zp, col, k)), cs.at[zp, far], cr.at[zp, far], block_of(z, x, 1 - k), me_v)

    def c_in(zp, far):
        col = 1 - x if far else x
        return remote(whole(block_of(zp, col, 1 - k)), cs.at[zp, far], cr.at[zp, far], block_of(z, x, 1 - k), me_v)

    def t_copy(i, frm=me_t):
        to = lax.rem(me_t + i, T)
        return pltpu.make_async_remote_copy(
            src_ref=tsend.at[pl.ds(pl.multiple_of(to * VS, VS), VS), :],
            dst_ref=tt.at[:, pl.ds(pl.multiple_of(frm * R, R), R)],
            send_sem=ts.at[i], recv_sem=tr.at[i], device_id=(to, me_v), device_id_type=MESH)

    def t_in(i):
        return t_copy(i, lax.rem(me_t - i + T, T))

    def sources(d):
        if d == 0:
            return [(z, None, None)]
        return [(jnp.maximum(z - d, 0), z - d >= 0, True), (jnp.minimum(z + d, L - 1), z + d < L, False)]

    def under(cond, f):
        if cond is None:
            f()
        else:
            pl.when(cond)(f)

    def arrive(d):
        for zp, cond, up in sources(d):
            def f(zp=zp, up=up):
                if d > 0:
                    z_copy(zp, up).wait_recv()
                if d == 0 or up:
                    pl.when(z + 1 < L)(lambda: z_copy(zp, True).start())
                if d == 0 or not up:
                    pl.when(z > 0)(lambda: z_copy(zp, False).start())
                x_copy(zp).start()
                if d == 0:
                    c_copy(zp, 0).start()
                else:
                    for j in range(1, V):
                        y_copy(zp, 0, j).start()
            under(cond, f)

    def crossed(d):
        for zp, cond, up in sources(d):
            def f(zp=zp):
                x_in(zp).wait_recv()
                for j in range(1, V):
                    y_copy(zp, 1, j).start()
            under(cond, f)

    def gathered(d):
        for zp, cond, up in sources(d):
            def f(zp=zp):
                if d > 0:
                    for j in range(1, V):
                        y_in(zp, 0, j).wait_recv()
                    c_copy(zp, 0).start()
                for j in range(1, V):
                    y_in(zp, 1, j).wait_recv()
                c_copy(zp, 1).start()
            under(cond, f)

    def t_start(i, c):
        to_z = lax.rem(me_t + i, T) // 4
        far = to_z != z
        pl.when(far if c else jnp.logical_not(far))(lambda: t_copy(i).start())

    def t_starts(across):
        def go(i, c):
            t_start(i, across)
            return c
        lax.fori_loop(1, T, go, 0)

    HC = 256

    def hot_chunk(j):
        row = trow_ref[:, pl.ds(pl.multiple_of(j * HC, HC), HC)]
        return jnp.where(lax.broadcasted_iota(jnp.int32, (TOK, HC), 0) == row, 1.0, 0.0).astype(BF16)

    keep_hot = hot.shape[1] == TOK

    def turn_step(j, c):
        at = pl.ds(pl.multiple_of(j * VS, VS), VS)
        tsend[at, :] = tload[:, at].astype(F32).T.astype(BF16)
        return c

    arrive(0)
    own_w.wait()
    wt[...] = wbuf[...].astype(F32).T.astype(BF16)
    arrive(1)
    own_t.wait()
    lax.fori_loop(0, T, turn_step, 0)
    t_starts(True)
    t_starts(False)
    crossed(0)
    for d in range(2, L):
        arrive(d)
        crossed(d - 1)
        gathered(d - 2)
    mine = pl.ds(pl.multiple_of(me_t * R, R), R)
    tt[:, mine] = tsend[pl.ds(pl.multiple_of(me_t * VS, VS), VS), :]
    if keep_hot:
        def hot_step(j, c):
            hot[:, pl.ds(pl.multiple_of(j * HC, HC), HC)] = hot_chunk(j)
            return c
        lax.fori_loop(0, TOK // HC // 2, hot_step, 0)
    crossed(L - 1)
    gathered(L - 2)
    if keep_hot:
        lax.fori_loop(TOK // HC // 2, TOK // HC, hot_step, 0)
    gathered(L - 1)

    CH = 4 * R

    def c_wait(zp, c):
        c_in(zp, 0).wait_recv()
        c_in(zp, 1).wait_recv()
        return c

    lax.fori_loop(0, L, c_wait, 0)

    def logit_step(zp, c):
        at = pl.ds(pl.multiple_of(zp * CH, CH), CH)
        out = lax.dot_general(wt[...], hbuf[at, :], (((1,), (1,)), ((), ())), preferred_element_type=F32)
        logits[:, at] = out
        peak = jnp.max(out, axis=0, keepdims=True)
        lse = peak + jnp.log(jnp.sum(jnp.exp(out - peak), axis=0, keepdims=True))
        for q in range(CH // 128):
            xl[0, pl.ds(zp * (CH // 128) + q, 1), :] = lse[:, q * 128:(q + 1) * 128]

        return c

    lax.fori_loop(0, L, logit_step, 0)

    def stat_copy(buf, s, r, i):
        to = lax.rem(me + i, N)
        return pltpu.make_async_remote_copy(
            src_ref=buf.at[0], dst_ref=buf.at[i], send_sem=s.at[i], recv_sem=r.at[i],
            device_id=(to // V, lax.rem(to, V)), device_id_type=MESH)

    def stat_start(buf, s, r):
        def go(i, c):
            stat_copy(buf, s, r, i).start()
            return c
        lax.fori_loop(1, N, go, 0)

    def stat_wait(buf, s, r):
        def go(i, c):
            stat_copy(buf, s, r, i).wait_recv()
            return c
        lax.fori_loop(1, N, go, 0)

    stat_start(xl, ls, lr)

    def t_wait(i, c):
        t_in(i).wait_recv()
        return c

    lax.fori_loop(1, T, t_wait, 0)

    stat_wait(xl, ls, lr)
    peak = jnp.max(xl[...], axis=0)
    comb[...] = peak + jnp.log(jnp.sum(jnp.exp(xl[...] - peak[None]), axis=0))

    for j in range(TOK // HC):
        pick = hot[:, j * HC:(j + 1) * HC] if keep_hot else hot_chunk(j)
        aligned = jnp.dot(tt[...], pick, preferred_element_type=F32)
        for q in range(HC // 128):
            row = j * (HC // 128) + q
            at = slice(row * 128, (row + 1) * 128)
            log_student = logits[:, at] - comb[row:row + 1, :]
            s = jnp.exp(log_student)
            log_mix = jnp.log(0.5 * aligned[:, q * 128:(q + 1) * 128] + 0.5 * s)
            g = 0.5 * (log_student - log_mix)
            logits[:, at] = g
            student[:, at] = s
            xc[0, row:row + 1, :] = jnp.sum(s * g, axis=0, keepdims=True)

    stat_start(xc, es, er)
    stat_wait(xc, es, er)
    comb[...] = jnp.sum(xc[...], axis=0)

    count = lax.fori_loop(0, TOK // SEQ_LEN, lambda j, c: c + len_ref[j], jnp.int32(0))
    grad_scale = loss_scale / jnp.full((1, SEQ_LEN), count, jnp.int32).astype(F32)
    slot = lax.broadcasted_iota(jnp.int32, (1, SEQ_LEN), 1)

    def dlogit_step(j, c):
        at = pl.ds(pl.multiple_of(j * SEQ_LEN, SEQ_LEN), SEQ_LEN)
        scale = jnp.where(slot < len_ref[j], grad_scale, 0.0)
        d = (scale * student[:, at]) * (logits[:, at] - comb[pl.ds(j, 1), :])
        dt[:, at] = d.astype(BF16)
        return c

    lax.fori_loop(0, TOK // 128, dlogit_step, 0)

    GC = 256

    for j in range(D // GC):
        at = slice(j * GC, (j + 1) * GC)
        g = jnp.dot(dt[...], hbuf[:, at], preferred_element_type=F32)
        out_ref[at, :] = g.T.astype(BF16)

    def drain_stats(i, c):
        stat_copy(xl, ls, lr, i).wait_send()
        stat_copy(xc, es, er, i).wait_send()
        return c

    lax.fori_loop(1, N, drain_stats, 0)

    def drain_teacher(i, c):
        t_copy(i).wait_send()
        return c

    lax.fori_loop(1, T, drain_teacher, 0)

    def drain_hidden(zp, c):
        pl.when((z + 1 < L) & (zp <= z))(lambda: z_copy(zp, True).wait_send())
        pl.when((z > 0) & (zp >= z))(lambda: z_copy(zp, False).wait_send())
        x_copy(zp).wait_send()
        for j in range(1, V):
            y_copy(zp, 1, j).wait_send()
            pl.when(zp != z)(lambda: y_copy(zp, 0, j).wait_send())
        c_copy(zp, 0).wait_send()
        c_copy(zp, 1).wait_send()
        return c

    lax.fori_loop(0, L, drain_hidden, 0)


def per_device(T, V, hidden, head_weight, teacher_probs, teacher_row, lengths):
    R, D = hidden.shape
    VS = head_weight.shape[1]
    TOK = T * R
    N = T * V
    L = T // 4
    vm = pl.BlockSpec(memory_space=pltpu.VMEM)
    anyspace = pl.BlockSpec(memory_space=pl.ANY)
    dma = pltpu.SemaphoreType.DMA
    return pl.pallas_call(
        functools.partial(head_kernel, T, V),
        out_shape=jax.ShapeDtypeStruct((D, VS), BF16),
        in_specs=[anyspace, anyspace, anyspace, vm, pl.BlockSpec(memory_space=pltpu.SMEM)],
        out_specs=vm,
        scratch_shapes=[
            pltpu.VMEM((D, VS), BF16),
            pltpu.VMEM((TOK, TOK) if TOK * TOK <= 2**22 else (16, 128), BF16),
            pltpu.VMEM((TOK, D), BF16),
            pltpu.VMEM((R, T * VS), BF16),
            pltpu.VMEM((T * VS, R), BF16),
            pltpu.VMEM((VS, TOK), BF16),
            pltpu.VMEM((VS, D), BF16),
            pltpu.VMEM((VS, TOK), F32),
            pltpu.VMEM((VS, TOK), F32),
            pltpu.VMEM((VS, TOK), BF16),
            pltpu.VMEM((N, TOK // 128, 128), F32),
            pltpu.VMEM((N, TOK // 128, 128), F32),
            pltpu.VMEM((TOK // 128, 128), F32),
            dma((3,)),
            dma((L, 2)), dma((L,)),
            dma((L,)), dma((L,)),
            dma((L, 2, V)), dma((L, 2, V)),
            dma((L, 2)), dma((L, 2)),
            dma((T,)), dma((T,)),
            dma((N,)), dma((N,)),
            dma((N,)), dma((N,)),
        ],
        compiler_params=pltpu.CompilerParams(
            collective_id=0, has_side_effects=True, vmem_limit_bytes=60 * 1024 * 1024
        ),
        cost_estimate=pl.CostEstimate(
            flops=6 * TOK * D * VS, bytes_accessed=4 * TOK * D, transcendentals=4 * TOK * VS
        ),
        name="head_grad",
    )(hidden, head_weight, teacher_probs, teacher_row.reshape(1, TOK), lengths)


def solution(mesh):
    return jax.shard_map(
        functools.partial(per_device, mesh.shape["tok"], mesh.shape["voc"]),
        mesh=mesh,
        in_specs=(P("tok", None), P(None, ("voc", "tok")), P("tok", "voc"), P(), P()),
        out_specs=P(None, ("voc", "tok")),
        check_vma=False,
    )
```

```python
import functools

import jax
import jax.numpy as jnp
from jax import lax
from jax.experimental import pallas as pl
from jax.experimental.pallas import tpu as pltpu
from jax.sharding import PartitionSpec as P

SEQ_LEN = 128
loss_scale = 1048576.0
MESH = pl.DeviceIdType.MESH
F32 = jnp.float32
BF16 = jnp.bfloat16


def head_kernel(
    T, V,
    h_hbm, w_hbm, t_hbm, trow_ref, len_ref, out_ref,
    wbuf, hot, hbuf, tload, tsend, tt, wt, logits, student, dt, xl, xc, comb,
    loc_sem, zs, zr, xs, xr, ys, yr, cs, cr, ts, tr, ls, lr, es, er,
):
    N = T * V
    R, D = h_hbm.shape
    VS = w_hbm.shape[1]
    TOK = T * R
    L = T // 4
    part = R // V
    me_t, me_v = lax.axis_index("tok"), lax.axis_index("voc")
    me = me_t * V + me_v
    k = lax.rem(me_t, 2)
    x = lax.rem(me_t // 2, 2)
    z = me_t // 4

    def block_of(zz, xx, kk):
        return (zz * 2 + xx) * 2 + kk

    own_h = pltpu.make_async_copy(h_hbm, hbuf.at[pl.ds(pl.multiple_of(me_t * R, R), R), :], loc_sem.at[0])
    own_h.start()
    own_t = pltpu.make_async_copy(t_hbm, tload, loc_sem.at[1])
    own_t.start()

    own_w = pltpu.make_async_copy(w_hbm, wbuf, loc_sem.at[2])
    own_w.start()

    barrier = pltpu.get_barrier_semaphore()

    def greet(i, c):
        to = lax.rem(me + i, N)
        pl.semaphore_signal(barrier, inc=1, device_id=(to // V, lax.rem(to, V)), device_id_type=MESH)
        return c

    lax.fori_loop(1, N, greet, 0)
    own_h.wait()
    pl.semaphore_wait(barrier, N - 1)

    def rows(n, p):
        return hbuf.at[pl.ds(pl.multiple_of(n * R + p * part, part), part), :]

    def whole(n):
        return hbuf.at[pl.ds(pl.multiple_of(n * R, R), R), :]

    def remote(ref, s_sem, r_sem, tok, voc):
        return pltpu.make_async_remote_copy(
            src_ref=ref, dst_ref=ref, send_sem=s_sem, recv_sem=r_sem,
            device_id=(tok, voc), device_id_type=MESH)

    def z_copy(zp, up):
        to = jnp.minimum(z + 1, L - 1) if up else jnp.maximum(z - 1, 0)
        return remote(rows(block_of(zp, x, k), me_v), zs.at[zp, 0 if up else 1], zr.at[zp],
                      block_of(to, x, k), me_v)

    def x_copy(zp):
        return remote(rows(block_of(zp, x, k), me_v), xs.at[zp], xr.at[zp], block_of(z, 1 - x, k), me_v)

    def x_in(zp):
        return remote(rows(block_of(zp, 1 - x, k), me_v), xs.at[zp], xr.at[zp], block_of(z, 1 - x, k), me_v)

    def y_copy(zp, far, j):
        col = 1 - x if far else x
        return remote(rows(block_of(zp, col, k), me_v), ys.at[zp, far, j], yr.at[zp, far, j],
                      me_t, lax.rem(me_v + j, V))

    def y_in(zp, far, j):
        col = 1 - x if far else x
        return remote(rows(block_of(zp, col, k), lax.rem(me_v - j + V, V)), ys.at[zp, far, j], yr.at[zp, far, j],
                      me_t, lax.rem(me_v + j, V))

    def c_copy(zp, far):
        col = 1 - x if far else x
        return remote(whole(block_of(zp, col, k)), cs.at[zp, far], cr.at[zp, far], block_of(z, x, 1 - k), me_v)

    def c_in(zp, far):
        col = 1 - x if far else x
        return remote(whole(block_of(zp, col, 1 - k)), cs.at[zp, far], cr.at[zp, far], block_of(z, x, 1 - k), me_v)

    def t_copy(i, frm=me_t):
        to = lax.rem(me_t + i, T)
        return pltpu.make_async_remote_copy(
            src_ref=tsend.at[pl.ds(pl.multiple_of(to * VS, VS), VS), :],
            dst_ref=tt.at[:, pl.ds(pl.multiple_of(frm * R, R), R)],
            send_sem=ts.at[i], recv_sem=tr.at[i], device_id=(to, me_v), device_id_type=MESH)

    def t_in(i):
        return t_copy(i, lax.rem(me_t - i + T, T))

    def sources(d):
        if d == 0:
            return [(z, None, None)]
        return [(jnp.maximum(z - d, 0), z - d >= 0, True), (jnp.minimum(z + d, L - 1), z + d < L, False)]

    def under(cond, f):
        if cond is None:
            f()
        else:
            pl.when(cond)(f)

    def arrive(d):
        for zp, cond, up in sources(d):
            def f(zp=zp, up=up):
                if d > 0:
                    z_copy(zp, up).wait_recv()
                if d == 0 or up:
                    pl.when(z + 1 < L)(lambda: z_copy(zp, True).start())
                if d == 0 or not up:
                    pl.when(z > 0)(lambda: z_copy(zp, False).start())
                x_copy(zp).start()
                if d == 0:
                    c_copy(zp, 0).start()
                else:
                    for j in range(1, V):
                        y_copy(zp, 0, j).start()
            under(cond, f)

    def crossed(d):
        for zp, cond, up in sources(d):
            def f(zp=zp):
                x_in(zp).wait_recv()
                for j in range(1, V):
                    y_copy(zp, 1, j).start()
            under(cond, f)

    def gathered(d):
        for zp, cond, up in sources(d):
            def f(zp=zp):
                if d > 0:
                    for j in range(1, V):
                        y_in(zp, 0, j).wait_recv()
                    c_copy(zp, 0).start()
                for j in range(1, V):
                    y_in(zp, 1, j).wait_recv()
                c_copy(zp, 1).start()
            under(cond, f)

    def t_start(i, c):
        to_z = lax.rem(me_t + i, T) // 4
        far = to_z != z
        pl.when(far if c else jnp.logical_not(far))(lambda: t_copy(i).start())

    def t_starts(across):
        def go(i, c):
            t_start(i, across)
            return c
        lax.fori_loop(1, T, go, 0)

    HC = 256

    def hot_chunk(j):
        row = trow_ref[:, pl.ds(pl.multiple_of(j * HC, HC), HC)]
        return jnp.where(lax.broadcasted_iota(jnp.int32, (TOK, HC), 0) == row, 1.0, 0.0).astype(BF16)

    keep_hot = hot.shape[1] == TOK

    def turn_step(j, c):
        at = pl.ds(pl.multiple_of(j * VS, VS), VS)
        tsend[at, :] = tload[:, at].astype(F32).T.astype(BF16)
        return c

    arrive(0)
    arrive(1)
    own_t.wait()
    lax.fori_loop(0, T, turn_step, 0)
    t_starts(True)
    t_starts(False)
    crossed(0)
    for d in range(2, L):
        arrive(d)
        crossed(d - 1)
        gathered(d - 2)
    own_w.wait()
    wt[...] = wbuf[...].astype(F32).T.astype(BF16)
    mine = pl.ds(pl.multiple_of(me_t * R, R), R)
    tt[:, mine] = tsend[pl.ds(pl.multiple_of(me_t * VS, VS), VS), :]
    if keep_hot:
        def hot_step(j, c):
            hot[:, pl.ds(pl.multiple_of(j * HC, HC), HC)] = hot_chunk(j)
            return c
        lax.fori_loop(0, TOK // HC // 2, hot_step, 0)
    crossed(L - 1)
    gathered(L - 2)
    if keep_hot:
        lax.fori_loop(TOK // HC // 2, TOK // HC, hot_step, 0)
    gathered(L - 1)

    CH = 4 * R

    def c_wait(zp, c):
        c_in(zp, 0).wait_recv()
        c_in(zp, 1).wait_recv()
        return c

    lax.fori_loop(0, L, c_wait, 0)

    def logit_step(zp, c):
        at = pl.ds(pl.multiple_of(zp * CH, CH), CH)
        out = lax.dot_general(wt[...], hbuf[at, :], (((1,), (1,)), ((), ())), preferred_element_type=F32)
        logits[:, at] = out
        peak = jnp.max(out, axis=0, keepdims=True)
        lse = peak + jnp.log(jnp.sum(jnp.exp(out - peak), axis=0, keepdims=True))
        for q in range(CH // 128):
            xl[0, pl.ds(zp * (CH // 128) + q, 1), :] = lse[:, q * 128:(q + 1) * 128]

        return c

    lax.fori_loop(0, L, logit_step, 0)

    def stat_copy(buf, s, r, i):
        to = lax.rem(me + i, N)
        return pltpu.make_async_remote_copy(
            src_ref=buf.at[0], dst_ref=buf.at[i], send_sem=s.at[i], recv_sem=r.at[i],
            device_id=(to // V, lax.rem(to, V)), device_id_type=MESH)

    def stat_start(buf, s, r):
        def go(i, c):
            stat_copy(buf, s, r, i).start()
            return c
        lax.fori_loop(1, N, go, 0)

    def stat_wait(buf, s, r):
        def go(i, c):
            stat_copy(buf, s, r, i).wait_recv()
            return c
        lax.fori_loop(1, N, go, 0)

    stat_start(xl, ls, lr)

    def t_wait(i, c):
        t_in(i).wait_recv()
        return c

    lax.fori_loop(1, T, t_wait, 0)

    stat_wait(xl, ls, lr)
    peak = jnp.max(xl[...], axis=0)
    comb[...] = peak + jnp.log(jnp.sum(jnp.exp(xl[...] - peak[None]), axis=0))

    for j in range(TOK // HC):
        pick = hot[:, j * HC:(j + 1) * HC] if keep_hot else hot_chunk(j)
        aligned = jnp.dot(tt[...], pick, preferred_element_type=F32)
        for q in range(HC // 128):
            row = j * (HC // 128) + q
            at = slice(row * 128, (row + 1) * 128)
            log_student = logits[:, at] - comb[row:row + 1, :]
            s = jnp.exp(log_student)
            log_mix = jnp.log(0.5 * aligned[:, q * 128:(q + 1) * 128] + 0.5 * s)
            g = 0.5 * (log_student - log_mix)
            logits[:, at] = g
            student[:, at] = s
            xc[0, row:row + 1, :] = jnp.sum(s * g, axis=0, keepdims=True)

    stat_start(xc, es, er)
    stat_wait(xc, es, er)
    comb[...] = jnp.sum(xc[...], axis=0)

    count = lax.fori_loop(0, TOK // SEQ_LEN, lambda j, c: c + len_ref[j], jnp.int32(0))
    grad_scale = loss_scale / jnp.full((1, SEQ_LEN), count, jnp.int32).astype(F32)
    slot = lax.broadcasted_iota(jnp.int32, (1, SEQ_LEN), 1)

    def dlogit_step(j, c):
        at = pl.ds(pl.multiple_of(j * SEQ_LEN, SEQ_LEN), SEQ_LEN)
        scale = jnp.where(slot < len_ref[j], grad_scale, 0.0)
        d = (scale * student[:, at]) * (logits[:, at] - comb[pl.ds(j, 1), :])
        dt[:, at] = d.astype(BF16)
        return c

    lax.fori_loop(0, TOK // 128, dlogit_step, 0)

    GC = 256

    for j in range(D // GC):
        at = slice(j * GC, (j + 1) * GC)
        g = jnp.dot(dt[...], hbuf[:, at], preferred_element_type=F32)
        out_ref[at, :] = g.T.astype(BF16)

    def drain_stats(i, c):
        stat_copy(xl, ls, lr, i).wait_send()
        stat_copy(xc, es, er, i).wait_send()
        return c

    lax.fori_loop(1, N, drain_stats, 0)

    def drain_teacher(i, c):
        t_copy(i).wait_send()
        return c

    lax.fori_loop(1, T, drain_teacher, 0)

    def drain_hidden(zp, c):
        pl.when((z + 1 < L) & (zp <= z))(lambda: z_copy(zp, True).wait_send())
        pl.when((z > 0) & (zp >= z))(lambda: z_copy(zp, False).wait_send())
        x_copy(zp).wait_send()
        for j in range(1, V):
            y_copy(zp, 1, j).wait_send()
            pl.when(zp != z)(lambda: y_copy(zp, 0, j).wait_send())
        c_copy(zp, 0).wait_send()
        c_copy(zp, 1).wait_send()
        return c

    lax.fori_loop(0, L, drain_hidden, 0)


def per_device(T, V, hidden, head_weight, teacher_probs, teacher_row, lengths):
    R, D = hidden.shape
    VS = head_weight.shape[1]
    TOK = T * R
    N = T * V
    L = T // 4
    vm = pl.BlockSpec(memory_space=pltpu.VMEM)
    anyspace = pl.BlockSpec(memory_space=pl.ANY)
    dma = pltpu.SemaphoreType.DMA
    return pl.pallas_call(
        functools.partial(head_kernel, T, V),
        out_shape=jax.ShapeDtypeStruct((D, VS), BF16),
        in_specs=[anyspace, anyspace, anyspace, vm, pl.BlockSpec(memory_space=pltpu.SMEM)],
        out_specs=vm,
        scratch_shapes=[
            pltpu.VMEM((D, VS), BF16),
            pltpu.VMEM((TOK, TOK) if TOK * TOK <= 2**22 else (16, 128), BF16),
            pltpu.VMEM((TOK, D), BF16),
            pltpu.VMEM((R, T * VS), BF16),
            pltpu.VMEM((T * VS, R), BF16),
            pltpu.VMEM((VS, TOK), BF16),
            pltpu.VMEM((VS, D), BF16),
            pltpu.VMEM((VS, TOK), F32),
            pltpu.VMEM((VS, TOK), F32),
            pltpu.VMEM((VS, TOK), BF16),
            pltpu.VMEM((N, TOK // 128, 128), F32),
            pltpu.VMEM((N, TOK // 128, 128), F32),
            pltpu.VMEM((TOK // 128, 128), F32),
            dma((3,)),
            dma((L, 2)), dma((L,)),
            dma((L,)), dma((L,)),
            dma((L, 2, V)), dma((L, 2, V)),
            dma((L, 2)), dma((L, 2)),
            dma((T,)), dma((T,)),
            dma((N,)), dma((N,)),
            dma((N,)), dma((N,)),
        ],
        compiler_params=pltpu.CompilerParams(
            collective_id=0, has_side_effects=True, vmem_limit_bytes=60 * 1024 * 1024
        ),
        cost_estimate=pl.CostEstimate(
            flops=6 * TOK * D * VS, bytes_accessed=4 * TOK * D, transcendentals=4 * TOK * VS
        ),
        name="head_grad",
    )(hidden, head_weight, teacher_probs, teacher_row.reshape(1, TOK), lengths)


def solution(mesh):
    return jax.shard_map(
        functools.partial(per_device, mesh.shape["tok"], mesh.shape["voc"]),
        mesh=mesh,
        in_specs=(P("tok", None), P(None, ("voc", "tok")), P("tok", "voc"), P(), P()),
        out_specs=P(None, ("voc", "tok")),
        check_vma=False,
    )
```
